256 devices in a mesh: depth: 2 (over core), row: 16 (over x, y), col: 8 (over z).
Axes of the slice: x: 4, y: 4, z: 8, core: 2. Of those that a mesh axis runs over, the one named last changes fastest.
Arguments:
- rhs: float32 [2, 6, 16384, 1024], P(None, None, ('row', 'col'), 'depth'), may hold values from -6 to 6
- panels: bfloat16 [2, 2, 6, 16384, 512], P(None, None, 'depth', ('row', 'col')), may hold values from -0.1875 to 0.1875
- inverses: bfloat16 [2, 2, 512, 512], replicated, as said below
Outputs:
- result: float32 [2, 6, 16384, 1024], P(None, None, ('row', 'col'), 'depth')
The draws below stay inside these ranges and needn't reach their ends.
Inputs may be any that keep to these rules, and one draw needn't show every extreme that they name: Each inverses[s] is a lower triangular complex block, nonzero on its diagonal.
All inputs are finite; a program needn't handle non-finite values.
Results may differ from the reference program's by a relative error of at most 0.0046.
Values may be sent and summed in bfloat16 or wider, within the bound.
No kernel may reach another device: no remote copies, remote signals or barrier semaphores. Data moves between devices by JAX's collectives and lax.ppermute only.
A program may use at most 128 MiB of HBM per device.

```python
import math
import jax
import jax.numpy as jnp

ORDER = 98304
NB = 512
PIECE = 128
STEPS = 2
RHS = 1024
CYCLES = 6
N_ROW = 16
N_COL = 8


def draw_inverses(key, part):
    key = jax.random.fold_in(key, 7)
    first_key, second_key, third_key = jax.random.split(key, 3)
    row_ids = jnp.arange(NB)[:, None]
    col_ids = jnp.arange(NB)[None, :]
    lower_mask = (col_ids < row_ids).astype(jnp.float32)
    identity = (col_ids == row_ids).astype(jnp.float32)
    noise = jax.random.normal(first_key, (STEPS, 2, NB, NB), jnp.float32)
    offdiag = noise * lower_mask * (1.0 / math.sqrt(NB))
    diag_real = jax.random.uniform(second_key, (STEPS, NB), jnp.float32, 0.6, 1.4)
    diag_imag = jax.random.uniform(third_key, (STEPS, NB), jnp.float32, -0.3, 0.3)
    diagonal = jnp.stack([diag_real[:, None, :] * identity, diag_imag[:, None, :] * identity], axis=1)
    return (offdiag + diagonal).astype(jnp.bfloat16)


def steps_of(rng, extent, pieces, low, top_value):
    factor_of, own = 1.0, jax.random.fold_in(rng, 6)
    for axis_at, shards_of in pieces:
        heights = jnp.exp(jax.random.uniform(jax.random.fold_in(own, axis_at), (shards_of,), jnp.float32, low / len(pieces), top_value / len(pieces)))
        factor_of = factor_of * jnp.repeat(heights, extent[axis_at] // shards_of).reshape([-1 if axis == axis_at else 1 for axis in range(len(extent))])
    return factor_of


def normal_values(stream_key, extent, width, reach, pieces=(), held_as=jnp.bfloat16):
    factor_of = steps_of(stream_key, extent, pieces, -0.22, 0.18) if pieces else 1.0
    array = jax.random.normal(stream_key, extent, jnp.float32) * width * factor_of
    return jnp.minimum(jnp.maximum(array, -reach), reach).astype(held_as)


def setup_inputs(seed: int = 0) -> dict:
    key_list = jax.random.split(jax.random.key(seed), 4)
    return {
        "rhs": normal_values(key_list[0], (2, CYCLES, N_ROW * N_COL * PIECE, RHS), 1.0, 6.0, ((2, 128), (3, 2)), jnp.float32),
        "panels": normal_values(key_list[1], (STEPS, 2, CYCLES, N_ROW * N_COL * PIECE, NB), (2 * NB) ** -0.5, 0.1875, ((2, 2), (3, 128))),
        "inverses": draw_inverses(jax.random.fold_in(key_list[3], 71), 0),
    }


def complex_dot(left_real, left_imag, right_real, right_imag):
    real_part = jnp.dot(left_real, right_real, preferred_element_type=jnp.float32) - jnp.dot(left_imag, right_imag, preferred_element_type=jnp.float32)
    imag_part = jnp.dot(left_real, right_imag, preferred_element_type=jnp.float32) + jnp.dot(left_imag, right_real, preferred_element_type=jnp.float32)
    return jnp.stack([real_part, imag_part])


def reference(rhs, panels, inverses):
    current = rhs.reshape(2, ORDER, RHS)
    matrix = panels.reshape(STEPS, 2, ORDER, NB)
    solutions = []
    for step_index in range(STEPS):
        block_rhs = current[:, step_index * NB:(step_index + 1) * NB].astype(jnp.bfloat16)
        solved = complex_dot(inverses[step_index, 0], inverses[step_index, 1], block_rhs[0], block_rhs[1])
        solutions.append(solved)
        solved_half = solved.astype(jnp.bfloat16)
        lower_start = (step_index + 1) * NB
        update = complex_dot(matrix[step_index, 0, lower_start:], matrix[step_index, 1, lower_start:], solved_half[0], solved_half[1])
        current = current.at[:, lower_start:].set(current[:, lower_start:] - update)
    for step_index in range(STEPS):
        current = current.at[:, step_index * NB:(step_index + 1) * NB].set(solutions[step_index])
    return current.reshape(rhs.shape)
```

```python
import jax
import jax.numpy as jnp
from jax import lax
from jax.experimental import pallas as pl
from jax.experimental.pallas import tpu as pltpu
from jax.sharding import PartitionSpec as P

BF = jnp.bfloat16
F32 = jnp.float32


def dot(left, right):
    return jnp.dot(left, right, preferred_element_type=F32)


def kernel(where_ref, recv_ref, other_ref, inv_ref, own_ref, swap_ref, rhs_ref, out_ref, diag, work, sol, full):
    depth = where_ref[0]
    position = where_ref[1]
    step = pl.program_id(0)
    lanes = pl.ds(pl.multiple_of(step * 128, 128), 128)

    @pl.when(step == 0)
    def _():
        for ref, which in ((recv_ref, depth), (other_ref, 1 - depth)):
            base = 128 if ref is recv_ref else 0
            for piece in range(4):
                h, w = piece // 2, piece % 2
                for r in range(16):
                    diag[which, piece * 128 + 16 * (r // 2) : piece * 128 + 16 * (r // 2) + 16, 256 * (r % 2) : 256 * (r % 2) + 256] = ref[
                        r, base + 16 * h : base + 16 * h + 16, 256 * w : 256 * w + 256
                    ]

    def put(ref, at, real, imag):
        rows = real.shape[0]
        ref[at : at + rows, 0:128] = real
        ref[at : at + rows, 128:256] = imag
        ref[512 + at : 512 + at + rows, 0:128] = -imag
        ref[512 + at : 512 + at + rows, 128:256] = real

    def block(s, part):
        return jnp.concatenate(
            [recv_ref[8 * part + rr, (4 * s + zz) * 16 : (4 * s + zz) * 16 + 16, lanes] for zz in range(4) for rr in range(8)], axis=0
        )

    def solve(s):
        top = dot(inv_ref[s, 0, :256, :256], work[0:256]) + dot(inv_ref[s, 1, :256, :256], work[512:768])
        low = dot(inv_ref[s, 0, 256:, :], work[0:512]) + dot(inv_ref[s, 1, 256:, :], work[512:1024])
        for at, value in ((0, top), (256, low)):
            full[s, at : at + 256] = value
            half = value.astype(BF)
            put(sol.at[s], at, half[:, :128], half[:, 128:])

    put(work, 0, block(0, 0), block(0, 1))
    solve(0)
    taken = dot(diag[0], sol[0, 0:512]) + dot(diag[1], sol[0, 512:1024])
    put(
        work,
        0,
        (block(1, 0).astype(F32) - taken[:, :128]).astype(BF),
        (block(1, 1).astype(F32) - taken[:, 128:]).astype(BF),
    )
    solve(1)
    for ref, first in ((own_ref, depth * 3), (swap_ref, 3 - depth * 3)):
        total = None
        for s in range(2):
            for part in range(2):
                term = dot(ref[s, part].reshape(384, 512), sol[s, 512 * part : 512 * part + 512])
                total = term if total is None else total + term
        for part in range(2):
            old = rhs_ref[part, pl.ds(first, 3)]
            out_ref[part, pl.ds(first, 3)] = old - total[:, 128 * part : 128 * part + 128].reshape(3, 128, 128)

    @pl.when(position < 8)
    def _():
        rows = pl.ds(pl.multiple_of((position % 4) * 128, 128), 128)
        for part in range(2):
            out_ref[part, 0] = full[position // 4, rows, 128 * part : 128 * part + 128]


def update(where, recv, other, inverses, own, swap, rhs):
    whole = pl.BlockSpec(memory_space=pltpu.VMEM)
    tile = pl.BlockSpec((2, 6, 128, 128), lambda i: (0, 0, 0, i))
    return pl.pallas_call(
        kernel,
        grid=(4,),
        in_specs=[pl.BlockSpec(memory_space=pltpu.SMEM)] + [whole] * 5 + [tile],
        out_specs=tile,
        out_shape=jax.ShapeDtypeStruct(rhs.shape, F32),
        scratch_shapes=[
            pltpu.VMEM((2, 512, 512), BF),
            pltpu.VMEM((1024, 256), BF),
            pltpu.VMEM((2, 1024, 256), BF),
            pltpu.VMEM((2, 512, 256), F32),
        ],
        compiler_params=pltpu.CompilerParams(vmem_limit_bytes=48 * 1024 * 1024),
        cost_estimate=pl.CostEstimate(flops=6_400_000_000, bytes_accessed=12_000_000, transcendentals=0),
    )(where, recv, other, inverses, own, swap, rhs)


def per_device(rhs, panels, inverses):
    depth = lax.axis_index("depth")
    position = lax.axis_index(("row", "col"))
    where = jnp.stack([depth, position]).astype(jnp.int32)
    first = panels[0, :, 0]
    passed = lax.ppermute(first[1], "depth", [(0, 1), (1, 0)])
    mine = jnp.where(depth == 0, first[0], passed)
    swap = lax.ppermute(panels, "depth", [(0, 1), (1, 0)])
    rows = rhs[:, 0].astype(BF).reshape(16, 16, 512)
    mine = mine.reshape(8, 16, 2, 256).transpose(0, 2, 1, 3).reshape(16, 16, 256)
    dealt = lax.all_to_all(jnp.concatenate([rows, mine], axis=2), "row", 0, 0, tiled=True)[0]
    line = lax.all_to_all(jnp.broadcast_to(dealt, (8, 16, 768)), "col", 0, 0, tiled=True)
    tail = line[4:, :, 512:].reshape(2, 2, 16, 256).transpose(0, 2, 1, 3).reshape(32, 512)
    share = jnp.concatenate([line[:, :, :512].reshape(128, 512), tail], axis=0)
    recv = lax.all_to_all(jnp.broadcast_to(share, (16, 160, 512)), "row", 0, 0, tiled=True)
    other = lax.ppermute(recv[:, 128:], "depth", [(0, 1), (1, 0)])
    return update(where, recv, other, inverses, panels.reshape(2, 2, 3, 128, 512), swap, rhs)


def solution(mesh):
    return jax.shard_map(
        per_device,
        mesh=mesh,
        in_specs=(
            P(None, None, ("row", "col"), "depth"),
            P(None, None, "depth", ("row", "col"), None),
            P(),
        ),
        out_specs=P(None, None, ("row", "col"), "depth"),
        check_vma=False,
    )
```

```python
import jax
import jax.numpy as jnp
from jax import lax
from jax.experimental import pallas as pl
from jax.experimental.pallas import tpu as pltpu
from jax.sharding import PartitionSpec as P

BF = jnp.bfloat16
F32 = jnp.float32
SWAP = [(0, 1), (1, 0)]
AXES = ("depth", "row", "col")
SIDE = 4
SHIFTS = (0, 1, 3, 2)
TILES = 4


def place(depth, x, y, z):
    return (depth * 16 + (x % SIDE) * SIDE + y % SIDE) * 8 + z


def plane_groups():
    return [
        [place(d, c // 4, c % 4, z) if d == 0 else place(d, c % 4, c // 4, z) for c in range(16)] for d in range(2) for z in range(8)
    ]


def slow_groups():
    return [
        [place(d, m, o, z) if d == 0 else place(d, o, m, z) for m in range(4)] for d in range(2) for z in range(8) for o in range(4)
    ]


def fast_shift(by):
    return [
        (place(d, x, y, z), place(d, x, y + by, z) if d == 0 else place(d, x + by, y, z))
        for d in range(2)
        for x in range(4)
        for y in range(4)
        for z in range(8)
    ]


def dot(left, right):
    return jnp.dot(left, right, preferred_element_type=F32)


def fill(copies, sems, start=0):
    copies = [pltpu.make_async_copy(source, target, sems.at[start + i]) for i, (source, target) in enumerate(copies)]
    for copy in copies:
        copy.start()
    return copies


def matrices(s, depth, inv_ref, own_ref, swap_ref, inv, panel):
    copies = [(inv_ref.at[s, part, :, 256 * k : 256 * k + 256], inv.at[:, 512 * k + 256 * part : 512 * k + 256 * part + 256]) for k in range(2) for part in range(2)]
    return copies + [
        (ref.at[s, part], panel.at[pl.ds(first, 3), :, 512 * part : 512 * part + 512])
        for part in range(2)
        for ref, first in ((own_ref, depth * 3), (swap_ref, 3 - depth * 3))
    ]


def places(where_ref):
    depth, position = where_ref[0], where_ref[1]
    place_x, place_y = position >> 5, (position >> 3) & 3
    group = jnp.where(depth == 0, place_y, place_x)
    return depth, position, group, place_x + place_y - group


def put(ref, at, back, value):
    rows = value.shape[0]
    for j in range(TILES):
        real, imag = value[:, 256 * j : 256 * j + 128], value[:, 256 * j + 128 : 256 * j + 256]
        ref[at : at + rows, 256 * j : 256 * j + 128] = real
        ref[at : at + rows, 256 * j + 128 : 256 * j + 256] = imag
        ref[back : back + rows, 256 * j : 256 * j + 128] = -imag
        ref[back : back + rows, 256 * j + 128 : 256 * j + 256] = real


def block(held, s, k):
    return jnp.concatenate(
        [
            jnp.concatenate(
                [ref[m, ((4 * s + zz) * 2 + part) * 32 : ((4 * s + zz) * 2 + part) * 32 + 32, :] for zz in (2 * k, 2 * k + 1) for m in range(4)], axis=0
            )
            for ref in held
            for part in range(2)
        ],
        axis=1,
    )


def solve(inv, work, sol, piece, rows):
    value = dot(inv[:, 0:512], work[0:512])
    low = value[256:] + dot(inv[256:, 512:1024], work[512:1024])
    for at, part in ((0, value[:256]), (256, low)):
        put(sol, at, 512 + at, part.astype(BF))

        @pl.when((rows >> 8) == (at >> 8))
        def _():
            piece[...] = jnp.where((rows & 128) == 0, part[:128], part[128:])


def fill_diag(diag, halves, first):
    for half, shift in zip(halves, SHIFTS):
        at = pl.multiple_of(((first + 4 - shift) & 3) * 128, 128)
        for m in range(4):
            for zz in range(4):
                diag[zz * 128 + m * 32 : zz * 128 + m * 32 + 32, pl.ds(at, 128)] = half[m, zz * 32 : zz * 32 + 32, :]


def first_kernel(where_ref, h0, h1, h2, h3, inv_ref, own_ref, swap_ref, rhs_ref, sol, state, left, inv1, panel1, inv0, panel0, diag, work, piece, sems):
    depth, position, group, _ = places(where_ref)
    held = (h0, h1, h2, h3)
    loads = fill(matrices(0, depth, inv_ref, own_ref, swap_ref, inv0, panel0), sems)
    loads_rhs = fill(
        [(rhs_ref.at[:, :, :, pl.ds(pl.multiple_of(((group + 4 - shift) & 3) * 128, 128), 128)], state.at[j]) for j, shift in enumerate(SHIFTS)], sems, 8
    )
    loads_next = fill(matrices(1, depth, inv_ref, own_ref, swap_ref, inv1, panel1), sems, 12)
    for k in range(2):
        put(work, 512 * k, 512 * k + 256, block(held, 0, k))
    fill_diag(diag, [ref.at[:, 512:640] for ref in held], group)
    for load in loads[:4]:
        load.wait()
    solve(inv0, work, sol, piece, (position & 3) * 128)
    ours = pl.ds(pl.multiple_of(depth * 512, 512), 512)
    for k in range(2):
        left[256 * k : 256 * k + 256] = block(held, 1, k).astype(F32) - dot(diag[256 * k : 256 * k + 256], sol[ours])
    for load in loads[4:] + loads_rhs:
        load.wait()
    for c in range(0, 6, 3):
        total = dot(panel0[c : c + 3].reshape(384, 1024), sol[...])
        for j in range(TILES):
            for part in range(2):
                at = 256 * j + 128 * part
                state[j, part, c : c + 3] = state[j, part, c : c + 3] - total[:, at : at + 128].reshape(3, 128, 128)

    @pl.when(position < 4)
    def _():
        for j in range(TILES):
            for part in range(2):
                at = 256 * j + 128 * part
                state[j, part, 0] = piece[:, at : at + 128]

    for load in loads_next:
        load.wait()


def second_kernel(where_ref, sol0, state, left, inv, panel, other_ref, out_ref, half, diag, work, sol, piece, new, sems, out_sems):
    depth, position, group, other_group = places(where_ref)
    (load,) = fill([(other_ref, half)], sems)
    load.wait()
    fill_diag(diag, [half.at[j] for j in range(TILES)], other_group)
    theirs = pl.ds(pl.multiple_of((1 - depth) * 512, 512), 512)
    for k in range(2):
        put(work, 512 * k, 512 * k + 256, (left[256 * k : 256 * k + 256] - dot(diag[256 * k : 256 * k + 256], sol0[theirs])).astype(BF))
    solve(inv, work, sol, piece, (position & 3) * 128)
    stores = []
    for c in range(0, 6, 2):
        total = dot(panel[c : c + 2].reshape(256, 1024), sol[...])
        for j in range(TILES):
            for part in range(2):
                at = 256 * j + 128 * part
                new[j, part, c : c + 2] = state[j, part, c : c + 2] - total[:, at : at + 128].reshape(2, 128, 128)
        if c == 0:
            @pl.when(position < 8)
            def _():
                for j in range(TILES):
                    for part in range(2):
                        at = 256 * j + 128 * part
                        new[j, part, 0] = jnp.where(position < 4, state[j, part, 0], piece[:, at : at + 128])

        stores += fill(
            [
                (new.at[j, :, c : c + 2], out_ref.at[:, c : c + 2, :, pl.ds(pl.multiple_of(((group + 4 - shift) & 3) * 128, 128), 128)])
                for j, shift in enumerate(SHIFTS)
            ],
            out_sems,
            2 * c,
        )
    for store in stores:
        store.wait()


def update(where, inverses, own, swap, rhs, held, other):
    smem = pl.BlockSpec(memory_space=pltpu.SMEM)
    hbm = pl.BlockSpec(memory_space=pl.ANY)
    vmem = pl.BlockSpec(memory_space=pltpu.VMEM)

    def call(body, cost, out_shape, scratch, *operands):
        return pl.pallas_call(
            body,
            in_specs=[smem] + [vmem if isinstance(value, list) else hbm for value in operands],
            out_specs=[vmem if isinstance(shape, pl.MemoryRef) else hbm for shape in out_shape],
            out_shape=out_shape,
            scratch_shapes=scratch,
            compiler_params=pltpu.CompilerParams(vmem_limit_bytes=14 * 1024 * 1024),
            cost_estimate=pl.CostEstimate(flops=cost, bytes_accessed=cost // 400, transcendentals=0),
        )(where, *[pltpu.with_memory_space_constraint(value[0], pltpu.VMEM) if isinstance(value, list) else value for value in operands])

    fixed = [pltpu.with_memory_space_constraint(value, pltpu.HBM) for value in (inverses, own, swap, rhs)]
    sol, state, left, inv, panel = call(
        first_kernel,
        3_000_000_000,
        [
            pltpu.VMEM((1024, 1024), BF),
            pltpu.VMEM((TILES, 2, 6, 128, 128), F32),
            pltpu.VMEM((512, 1024), F32),
            pltpu.VMEM((512, 1024), BF),
            pltpu.VMEM((6, 128, 1024), BF),
        ],
        [
            pltpu.VMEM((512, 1024), BF),
            pltpu.VMEM((6, 128, 1024), BF),
            pltpu.VMEM((512, 512), BF),
            pltpu.VMEM((1024, 1024), BF),
            pltpu.VMEM((128, 1024), F32),
            pltpu.SemaphoreType.DMA((20,)),
        ],
        *[[part] for part in held],
        *fixed,
    )
    (out,) = call(
        second_kernel,
        3_000_000_000,
        [jax.ShapeDtypeStruct(rhs.shape, F32)],
        [
            pltpu.VMEM((TILES, 4, 128, 128), BF),
            pltpu.VMEM((512, 512), BF),
            pltpu.VMEM((1024, 1024), BF),
            pltpu.VMEM((1024, 1024), BF),
            pltpu.VMEM((128, 1024), F32),
            pltpu.VMEM((TILES, 2, 6, 128, 128), F32),
            pltpu.SemaphoreType.DMA((1,)),
            pltpu.SemaphoreType.DMA((12,)),
        ],
        *[[value] for value in (sol, state, left, inv, panel)],
        other,
    )
    return out


def all_to_all(value, groups):
    return lax.all_to_all(value, AXES, 0, 0, axis_index_groups=groups, tiled=True)


def per_device(rhs, panels, inverses):
    depth = lax.axis_index("depth")
    position = lax.axis_index(("row", "col"))
    where = jnp.stack([depth, position]).astype(jnp.int32)
    first = panels[0, :, 0]
    passed = lax.ppermute(first[1], "depth", SWAP)
    mine = jnp.where(depth == 0, first[0], passed)
    swap = lax.ppermute(panels, "depth", SWAP)
    rows = rhs[:, 0].astype(BF).reshape(2, 4, 32, 4, 128).transpose(1, 3, 0, 2, 4).reshape(16, 64, 128)
    mine = mine.reshape(4, 32, 4, 128).transpose(0, 2, 1, 3).reshape(16, 32, 128)
    dealt = all_to_all(jnp.concatenate([rows, mine], axis=1), plane_groups())[0]
    line = lax.all_to_all(jnp.broadcast_to(dealt, (8, 96, 128)), "col", 0, 0, tiled=True)
    share = jnp.concatenate([line[:, :64].reshape(512, 128), line[4:, 64:].reshape(128, 128)], axis=0)
    held = all_to_all(jnp.broadcast_to(share, (4, 640, 128)), slow_groups())
    parts = [held] + [lax.ppermute(held, AXES, fast_shift(shift)) for shift in SHIFTS[1:]]
    other = lax.ppermute(jnp.stack([part[:, 512:] for part in parts]), "depth", SWAP)
    return update(where, inverses, panels, swap, rhs, parts, other)


def solution(mesh):
    return jax.shard_map(
        per_device,
        mesh=mesh,
        in_specs=(
            P(None, None, ("row", "col"), "depth"),
            P(None, None, "depth", ("row", "col"), None),
            P(),
        ),
        out_specs=P(None, None, ("row", "col"), "depth"),
        check_vma=False,
    )
```

```python
import jax
import jax.numpy as jnp
from jax import lax
from jax.experimental import pallas as pl
from jax.experimental.pallas import tpu as pltpu
from jax.sharding import PartitionSpec as P

BF = jnp.bfloat16
F32 = jnp.float32
SWAP = [(0, 1), (1, 0)]
AXES = ("depth", "row", "col")
SIDE = 4
SHIFTS = (0, 1, 3, 2)
TILES = 4


def place(depth, x, y, z):
    return (depth * 16 + (x % SIDE) * SIDE + y % SIDE) * 8 + z


def plane_groups():
    return [
        [place(d, c // 4, c % 4, z) if d == 0 else place(d, c % 4, c // 4, z) for c in range(16)] for d in range(2) for z in range(8)
    ]


def slow_groups():
    return [
        [place(d, m, o, z) if d == 0 else place(d, o, m, z) for m in range(4)] for d in range(2) for z in range(8) for o in range(4)
    ]


def fast_shift(by):
    return [
        (place(d, x, y, z), place(d, x, y + by, z) if d == 0 else place(d, x + by, y, z))
        for d in range(2)
        for x in range(4)
        for y in range(4)
        for z in range(8)
    ]


def dot(left, right):
    return jnp.dot(left, right, preferred_element_type=F32)


def fill(copies, sems, start=0):
    copies = [pltpu.make_async_copy(source, target, sems.at[start + i]) for i, (source, target) in enumerate(copies)]
    for copy in copies:
        copy.start()
    return copies


def matrix(s, inv_ref, inv):
    return [(inv_ref.at[s, part, :, 256 * k : 256 * k + 256], inv.at[:, 512 * k + 256 * part : 512 * k + 256 * part + 256]) for k in range(2) for part in range(2)]


def half_panel(s, ref, panel):
    return [(ref.at[s, part], panel.at[:, :, 512 * part : 512 * part + 512]) for part in range(2)]


def places(where_ref):
    depth, position = where_ref[0], where_ref[1]
    place_x, place_y = position >> 5, (position >> 3) & 3
    group = jnp.where(depth == 0, place_y, place_x)
    return depth, position, group, place_x + place_y - group


def put(ref, at, back, value):
    rows, columns = value.shape
    for j in range(0, columns, 256):
        real, imag = value[:, j : j + 128], value[:, j + 128 : j + 256]
        ref[at : at + rows, j : j + 128] = real
        ref[at : at + rows, j + 128 : j + 256] = imag
        ref[back : back + rows, j : j + 128] = -imag
        ref[back : back + rows, j + 128 : j + 256] = real


def block(held, s, k):
    return jnp.concatenate(
        [
            jnp.concatenate(
                [ref[m, ((4 * s + zz) * 2 + part) * 32 : ((4 * s + zz) * 2 + part) * 32 + 32, :] for zz in (2 * k, 2 * k + 1) for m in range(4)], axis=0
            )
            for ref in held
            for part in range(2)
        ],
        axis=1,
    )


def solve(inv, work, sol, piece, rows):
    value = dot(inv[:, 0:512], work[0:512])
    low = value[256:] + dot(inv[256:, 512:1024], work[512:1024])
    for at, part in ((0, value[:256]), (256, low)):
        put(sol, at, 512 + at, part.astype(BF))

        @pl.when((rows >> 8) == (at >> 8))
        def _():
            piece[...] = jnp.where((rows & 128) == 0, part[:128], part[128:])


def fill_diag(diag, halves, first):
    for half, shift in zip(halves, SHIFTS):
        at = pl.multiple_of(((first + 4 - shift) & 3) * 128, 128)
        for m in range(4):
            for zz in range(4):
                diag[zz * 128 + m * 32 : zz * 128 + m * 32 + 32, pl.ds(at, 128)] = half[m, zz * 32 : zz * 32 + 32, :]


def load_kernel(where_ref, h0, inv_ref, own_ref, rhs_ref, inv0, inv1, own0, own1, state, sol, piece, work, sems):
    depth, position, group, _ = places(where_ref)
    first = fill(matrix(0, inv_ref, inv0) + half_panel(0, own_ref, own0), sems)
    rest = [(rhs_ref.at[:, :, :, lanes(group, shift)], state.at[j]) for j, shift in enumerate(SHIFTS)]
    rest = fill(rest + matrix(1, inv_ref, inv1) + half_panel(1, own_ref, own1), sems, 6)
    for k in range(2):
        put(work, 512 * k, 512 * k + 256, block([h0], 0, k))
    for copy in first:
        copy.wait()
    solve(inv0, work, sol, piece, (position & 3) * 128)
    for copy in rest:
        copy.wait()
    less(state, state, own0, depth * 3, 0, 3, sol[...], 0)


def lanes(group, shift):
    return pl.ds(pl.multiple_of(((group + 4 - shift) & 3) * 128, 128), 128)


def less(new, old, panel, first, at, count, sol, tile):
    total = dot(panel[at : at + count].reshape(128 * count, 1024), sol)
    cycles = pl.ds(first + at, count)
    for j in range(total.shape[1] // 256):
        for part in range(2):
            place = 256 * j + 128 * part
            new[tile + j, part, cycles] = old[tile + j, part, cycles] - total[:, place : place + 128].reshape(count, 128, 128)


def first_kernel(where_ref, h0, h1, h2, h3, inv0, own0, old, known, known_piece, swap_ref, sol, state, left, swap1, swap0, diag, work, piece, sems):
    depth, position, group, _ = places(where_ref)
    held = (h0, h1, h2, h3)
    loads = fill(half_panel(0, swap_ref, swap0) + half_panel(1, swap_ref, swap1), sems)
    for k in range(2):
        put(work, 512 * k, 512 * k + 256, block(held[1:], 0, k))
    fill_diag(diag, [ref.at[:, 512:640] for ref in held], group)
    solve(inv0, work, sol.at[:, 256:], piece, (position & 3) * 128)
    sol[:, :256] = known[...]
    ours = pl.ds(pl.multiple_of(depth * 512, 512), 512)
    for k in range(2):
        left[256 * k : 256 * k + 256] = block(held, 1, k).astype(F32) - dot(diag[256 * k : 256 * k + 256], sol[ours])
    less(state, old, own0, depth * 3, 0, 3, sol[:, 256:], 1)
    state[0, :, pl.ds(depth * 3, 3)] = old[0, :, pl.ds(depth * 3, 3)]
    for load in loads:
        load.wait()
    less(state, old, swap0, 3 - depth * 3, 0, 3, sol[...], 0)

    @pl.when(position < 4)
    def _():
        for j in range(TILES):
            for part in range(2):
                at = 256 * j + 128 * part
                state[j, part, 0] = known_piece[:, at : at + 128] if j == 0 else piece[:, at - 256 : at - 128]


def second_kernel(where_ref, sol0, state, left, inv, own, swap, half, out_ref, diag, work, sol, piece, new, out_sems):
    depth, position, group, other_group = places(where_ref)
    fill_diag(diag, [half.at[j] for j in range(TILES)], other_group)
    theirs = pl.ds(pl.multiple_of((1 - depth) * 512, 512), 512)
    for k in range(2):
        put(work, 512 * k, 512 * k + 256, (left[256 * k : 256 * k + 256] - dot(diag[256 * k : 256 * k + 256], sol0[theirs])).astype(BF))
    solve(inv, work, sol, piece, (position & 3) * 128)
    stores = []
    for panel, first, at, count in ((own, depth * 3, 0, 2), (own, depth * 3, 2, 1), (swap, 3 - depth * 3, 0, 2), (swap, 3 - depth * 3, 2, 1)):
        less(new, state, panel, first, at, count, sol[...], 0)
        if at == 0:
            @pl.when((position < 8) & (first == 0))
            def _():
                for j in range(TILES):
                    for part in range(2):
                        place = 256 * j + 128 * part
                        new[j, part, 0] = jnp.where(position < 4, state[j, part, 0], piece[:, place : place + 128])

        cycles = pl.ds(first + at, count)
        stores += fill([(new.at[j, :, cycles], out_ref.at[:, cycles, :, lanes(group, shift)]) for j, shift in enumerate(SHIFTS)], out_sems, len(stores))
    for store in stores:
        store.wait()


def update(where, inverses, own, swap, rhs, held, other):
    smem = pl.BlockSpec(memory_space=pltpu.SMEM)
    hbm = pl.BlockSpec(memory_space=pl.ANY)
    vmem = pl.BlockSpec(memory_space=pltpu.VMEM)

    def call(body, cost, out_shape, scratch, *operands):
        return pl.pallas_call(
            body,
            in_specs=[smem] + [vmem if isinstance(value, list) else hbm for value in operands],
            out_specs=[vmem if isinstance(shape, pl.MemoryRef) else hbm for shape in out_shape],
            out_shape=out_shape,
            scratch_shapes=scratch,
            compiler_params=pltpu.CompilerParams(vmem_limit_bytes=14 * 1024 * 1024),
            cost_estimate=pl.CostEstimate(flops=cost, bytes_accessed=cost // 400, transcendentals=0),
        )(where, *[pltpu.with_memory_space_constraint(value[0], pltpu.VMEM) if isinstance(value, list) else value for value in operands])

    inverses, own, swap, rhs = [pltpu.with_memory_space_constraint(value, pltpu.HBM) for value in (inverses, own, swap, rhs)]
    inverse, half = pltpu.VMEM((512, 1024), BF), pltpu.VMEM((3, 128, 1024), BF)
    state = pltpu.VMEM((TILES, 2, 6, 128, 128), F32)
    inv0, inv1, own0, own1, old, known, piece = call(
        load_kernel,
        1_000_000_000,
        [inverse, inverse, half, half, state, pltpu.VMEM((1024, 256), BF), pltpu.VMEM((128, 256), F32)],
        [pltpu.VMEM((1024, 256), BF), pltpu.SemaphoreType.DMA((16,))],
        [held[0]],
        inverses,
        own,
        rhs,
    )
    sol, new, left, swap1 = call(
        first_kernel,
        60_000_000_000,
        [pltpu.VMEM((1024, 1024), BF), state, pltpu.VMEM((512, 1024), F32), half],
        [
            half,
            pltpu.VMEM((512, 512), BF),
            pltpu.VMEM((1024, 768), BF),
            pltpu.VMEM((128, 768), F32),
            pltpu.SemaphoreType.DMA((4,)),
        ],
        *[[value] for value in (*held, inv0, own0, old, known, piece)],
        swap,
    )
    (out,) = call(
        second_kernel,
        3_000_000_000,
        [jax.ShapeDtypeStruct(rhs.shape, F32)],
        [
            pltpu.VMEM((512, 512), BF),
            pltpu.VMEM((1024, 1024), BF),
            pltpu.VMEM((1024, 1024), BF),
            pltpu.VMEM((128, 1024), F32),
            state,
            pltpu.SemaphoreType.DMA((16,)),
        ],
        *[[value] for value in (sol, new, left, inv1, own1, swap1, other)],
    )
    return out


def all_to_all(value, groups):
    return lax.all_to_all(value, AXES, 0, 0, axis_index_groups=groups, tiled=True)


def per_device(rhs, panels, inverses):
    depth = lax.axis_index("depth")
    position = lax.axis_index(("row", "col"))
    where = jnp.stack([depth, position]).astype(jnp.int32)
    swap = lax.ppermute(panels, "depth", SWAP)
    mine = jnp.where(where[0] == 0, panels[0, 0, 0], swap[0, 1, 0])
    rows = rhs[:, 0].astype(BF).reshape(2, 4, 32, 4, 128).transpose(1, 3, 0, 2, 4).reshape(16, 64, 128)
    mine = mine.reshape(4, 32, 4, 128).transpose(0, 2, 1, 3).reshape(16, 32, 128)
    dealt = all_to_all(jnp.concatenate([rows, mine], axis=1), plane_groups())[0]
    line = lax.all_to_all(jnp.broadcast_to(dealt, (8, 96, 128)), "col", 0, 0, tiled=True)
    share = jnp.concatenate([line[:, :64].reshape(512, 128), line[4:, 64:].reshape(128, 128)], axis=0)
    held = all_to_all(jnp.broadcast_to(share, (4, 640, 128)), slow_groups())
    parts = [held] + [lax.ppermute(held, AXES, fast_shift(shift)) for shift in SHIFTS[1:]]
    other = lax.ppermute(jnp.stack([part[:, 512:] for part in parts]), "depth", SWAP)
    return update(where, inverses, panels, swap, rhs, parts, other)


def solution(mesh):
    return jax.shard_map(
        per_device,
        mesh=mesh,
        in_specs=(
            P(None, None, ("row", "col"), "depth"),
            P(None, None, "depth", ("row", "col"), None),
            P(),
        ),
        out_specs=P(None, None, ("row", "col"), "depth"),
        check_vma=False,
    )
```

```python
import jax
import jax.numpy as jnp
from jax import lax
from jax.experimental import pallas as pl
from jax.experimental.pallas import tpu as pltpu
from jax.sharding import PartitionSpec as P

BF = jnp.bfloat16
F32 = jnp.float32
SWAP = [(0, 1), (1, 0)]
AXES = ("depth", "row", "col")
SIDE = 4
SHIFTS = (0, 1, 3, 2)
TILES = 4


def place(depth, x, y, z):
    return (depth * 16 + (x % SIDE) * SIDE + y % SIDE) * 8 + z


def plane_groups():
    return [
        [place(d, c // 4, c % 4, z) if d == 0 else place(d, c % 4, c // 4, z) for c in range(16)] for d in range(2) for z in range(8)
    ]


def slow_groups():
    return [
        [place(d, m, o, z) if d == 0 else place(d, o, m, z) for m in range(4)] for d in range(2) for z in range(8) for o in range(4)
    ]


def fast_shift(by):
    return [
        (place(d, x, y, z), place(d, x, y + by, z) if d == 0 else place(d, x + by, y, z))
        for d in range(2)
        for x in range(4)
        for y in range(4)
        for z in range(8)
    ]


def dot(left, right):
    return jnp.dot(left, right, preferred_element_type=F32)


def fill(copies, sems, start=0):
    copies = [pltpu.make_async_copy(source, target, sems.at[start + i]) for i, (source, target) in enumerate(copies)]
    for copy in copies:
        copy.start()
    return copies


def matrix(s, inv_ref, inv):
    return [(inv_ref.at[s, part, :, 256 * k : 256 * k + 256], inv.at[:, 512 * k + 256 * part : 512 * k + 256 * part + 256]) for k in range(2) for part in range(2)]


def half_panel(s, ref, panel):
    return [(ref.at[s, part], panel.at[:, :, 512 * part : 512 * part + 512]) for part in range(2)]


def places(where_ref):
    depth, position = where_ref[0], where_ref[1]
    place_x, place_y = position >> 5, (position >> 3) & 3
    group = jnp.where(depth == 0, place_y, place_x)
    return depth, position, group, place_x + place_y - group


def put(ref, at, back, value):
    rows, columns = value.shape
    for j in range(0, columns, 256):
        real, imag = value[:, j : j + 128], value[:, j + 128 : j + 256]
        ref[at : at + rows, j : j + 128] = real
        ref[at : at + rows, j + 128 : j + 256] = imag
        ref[back : back + rows, j : j + 128] = -imag
        ref[back : back + rows, j + 128 : j + 256] = real


def block(held, s, k):
    return jnp.concatenate(
        [
            jnp.concatenate(
                [ref[m, ((4 * s + zz) * 2 + part) * 32 : ((4 * s + zz) * 2 + part) * 32 + 32, :] for zz in (2 * k, 2 * k + 1) for m in range(4)], axis=0
            )
            for ref in held
            for part in range(2)
        ],
        axis=1,
    )


def solve(inv, work, sol, piece, rows):
    value = dot(inv[:, 0:512], work[0:512])
    low = value[256:] + dot(inv[256:, 512:1024], work[512:1024])
    for at, part in ((0, value[:256]), (256, low)):
        put(sol, at, 512 + at, part.astype(BF))

        @pl.when((rows >> 8) == (at >> 8))
        def _():
            piece[...] = jnp.where((rows & 128) == 0, part[:128], part[128:])


def fill_diag(diag, halves, first):
    for half, shift in zip(halves, SHIFTS):
        at = pl.multiple_of(((first + 4 - shift) & 3) * 128, 128)
        for m in range(4):
            for zz in range(4):
                diag[zz * 128 + m * 32 : zz * 128 + m * 32 + 32, pl.ds(at, 128)] = half[m, zz * 32 : zz * 32 + 32, :]


def load_kernel(where_ref, h0, inv_ref, own_ref, swap_ref, rhs_ref, inv0, inv1, own, swap, state, sol, piece, work, sems):
    depth, position, group, _ = places(where_ref)
    first = fill(matrix(0, inv_ref, inv0) + half_panel(0, own_ref, own.at[0]) + half_panel(0, swap_ref, swap.at[0]), sems)
    rest = [(rhs_ref.at[:, :, :, lanes(group, shift)], state.at[j]) for j, shift in enumerate(SHIFTS)]
    rest = fill(rest + matrix(1, inv_ref, inv1) + half_panel(1, own_ref, own.at[1]) + half_panel(1, swap_ref, swap.at[1]), sems, 8)
    for k in range(2):
        put(work, 512 * k, 512 * k + 256, block([h0], 0, k))
    for copy in first:
        copy.wait()
    solve(inv0, work, sol, piece, (position & 3) * 128)
    for copy in rest:
        copy.wait()
    less(state, state, own.at[0], depth * 3, 0, 3, sol[...], 0)
    less(state, state, swap.at[0], 3 - depth * 3, 0, 3, sol[...], 0)


def lanes(group, shift):
    return pl.ds(pl.multiple_of(((group + 4 - shift) & 3) * 128, 128), 128)


def less(new, old, panel, first, at, count, sol, tile):
    total = dot(panel[at : at + count].reshape(128 * count, 1024), sol)
    cycles = pl.ds(first + at, count)
    for j in range(total.shape[1] // 256):
        for part in range(2):
            place = 256 * j + 128 * part
            new[tile + j, part, cycles] = old[tile + j, part, cycles] - total[:, place : place + 128].reshape(count, 128, 128)


def first_kernel(where_ref, h0, h1, h2, h3, inv0, own, swap, old, known, known_piece, sol, state, left, diag, work, piece):
    depth, position, group, _ = places(where_ref)
    held = (h0, h1, h2, h3)
    for k in range(2):
        put(work, 512 * k, 512 * k + 256, block(held[1:], 0, k))
    fill_diag(diag, [ref.at[:, 512:640] for ref in held], group)
    solve(inv0, work, sol.at[:, 256:], piece, (position & 3) * 128)
    sol[:, :256] = known[...]
    ours = pl.ds(pl.multiple_of(depth * 512, 512), 512)
    for k in range(2):
        left[256 * k : 256 * k + 256] = block(held, 1, k).astype(F32) - dot(diag[256 * k : 256 * k + 256], sol[ours])
    state[0] = old[0]
    less(state, old, own.at[0], depth * 3, 0, 3, sol[:, 256:], 1)
    less(state, old, swap.at[0], 3 - depth * 3, 0, 3, sol[:, 256:], 1)

    @pl.when(position < 4)
    def _():
        for j in range(TILES):
            for part in range(2):
                at = 256 * j + 128 * part
                state[j, part, 0] = known_piece[:, at : at + 128] if j == 0 else piece[:, at - 256 : at - 128]


def second_kernel(where_ref, sol0, state, left, inv, own, swap, half, out_ref, diag, work, sol, piece, new, out_sems):
    depth, position, group, other_group = places(where_ref)
    fill_diag(diag, [half.at[j] for j in range(TILES)], other_group)
    theirs = pl.ds(pl.multiple_of((1 - depth) * 512, 512), 512)
    for k in range(2):
        put(work, 512 * k, 512 * k + 256, (left[256 * k : 256 * k + 256] - dot(diag[256 * k : 256 * k + 256], sol0[theirs])).astype(BF))
    solve(inv, work, sol, piece, (position & 3) * 128)
    stores = []
    for panel, first, at, count in ((own, depth * 3, 0, 2), (own, depth * 3, 2, 1), (swap, 3 - depth * 3, 0, 2), (swap, 3 - depth * 3, 2, 1)):
        less(new, state, panel.at[1], first, at, count, sol[...], 0)
        if at == 0:
            @pl.when((position < 8) & (first == 0))
            def _():
                for j in range(TILES):
                    for part in range(2):
                        place = 256 * j + 128 * part
                        new[j, part, 0] = jnp.where(position < 4, state[j, part, 0], piece[:, place : place + 128])

        cycles = pl.ds(first + at, count)
        stores += fill([(new.at[j, :, cycles], out_ref.at[:, cycles, :, lanes(group, shift)]) for j, shift in enumerate(SHIFTS)], out_sems, len(stores))
    for store in stores:
        store.wait()


def update(where, inverses, own, swap, rhs, held, other):
    smem = pl.BlockSpec(memory_space=pltpu.SMEM)
    hbm = pl.BlockSpec(memory_space=pl.ANY)
    vmem = pl.BlockSpec(memory_space=pltpu.VMEM)

    def call(body, cost, out_shape, scratch, *operands):
        return pl.pallas_call(
            body,
            in_specs=[smem] + [vmem if isinstance(value, list) else hbm for value in operands],
            out_specs=[vmem if isinstance(shape, pl.MemoryRef) else hbm for shape in out_shape],
            out_shape=out_shape,
            scratch_shapes=scratch,
            compiler_params=pltpu.CompilerParams(vmem_limit_bytes=14 * 1024 * 1024),
            cost_estimate=pl.CostEstimate(flops=cost, bytes_accessed=cost // 400, transcendentals=0),
        )(where, *[pltpu.with_memory_space_constraint(value[0], pltpu.VMEM) if isinstance(value, list) else value for value in operands])

    inverses, own, swap, rhs = [pltpu.with_memory_space_constraint(value, pltpu.HBM) for value in (inverses, own, swap, rhs)]
    inverse, half = pltpu.VMEM((512, 1024), BF), pltpu.VMEM((2, 3, 128, 1024), BF)
    state = pltpu.VMEM((TILES, 2, 6, 128, 128), F32)
    inv0, inv1, own, swap, old, known, piece = call(
        load_kernel,
        1_000_000_000,
        [inverse, inverse, half, half, state, pltpu.VMEM((1024, 256), BF), pltpu.VMEM((128, 256), F32)],
        [pltpu.VMEM((1024, 256), BF), pltpu.SemaphoreType.DMA((20,))],
        [held[0]],
        inverses,
        own,
        swap,
        rhs,
    )
    sol, new, left = call(
        first_kernel,
        60_000_000_000,
        [pltpu.VMEM((1024, 1024), BF), state, pltpu.VMEM((512, 1024), F32)],
        [
            pltpu.VMEM((512, 512), BF),
            pltpu.VMEM((1024, 768), BF),
            pltpu.VMEM((128, 768), F32),
        ],
        *[[value] for value in (*held, inv0, own, swap, old, known, piece)],
    )
    (out,) = call(
        second_kernel,
        3_000_000_000,
        [jax.ShapeDtypeStruct(rhs.shape, F32)],
        [
            pltpu.VMEM((512, 512), BF),
            pltpu.VMEM((1024, 1024), BF),
            pltpu.VMEM((1024, 1024), BF),
            pltpu.VMEM((128, 1024), F32),
            state,
            pltpu.SemaphoreType.DMA((16,)),
        ],
        *[[value] for value in (sol, new, left, inv1, own, swap, other)],
    )
    return out


def all_to_all(value, groups):
    return lax.all_to_all(value, AXES, 0, 0, axis_index_groups=groups, tiled=True)


def per_device(rhs, panels, inverses):
    depth = lax.axis_index("depth")
    position = lax.axis_index(("row", "col"))
    where = jnp.stack([depth, position]).astype(jnp.int32)
    swap = lax.ppermute(panels, "depth", SWAP)
    mine = jnp.where(where[0] == 0, lax.optimization_barrier(panels[0, 0, 0]), swap[0, 1, 0])
    rows = rhs[:, 0].astype(BF).reshape(2, 4, 32, 4, 128).transpose(1, 3, 0, 2, 4).reshape(16, 64, 128)
    mine = mine.reshape(4, 32, 4, 128).transpose(0, 2, 1, 3).reshape(16, 32, 128)
    dealt = all_to_all(jnp.concatenate([rows, mine], axis=1), plane_groups())[0]
    line = lax.all_to_all(jnp.broadcast_to(dealt, (8, 96, 128)), "col", 0, 0, tiled=True)
    share = jnp.concatenate([line[:, :64].reshape(512, 128), line[4:, 64:].reshape(128, 128)], axis=0)
    held = all_to_all(jnp.broadcast_to(share, (4, 640, 128)), slow_groups())
    parts = [held] + [lax.ppermute(held, AXES, fast_shift(shift)) for shift in SHIFTS[1:]]
    other = lax.ppermute(jnp.stack([part[:, 512:] for part in parts]), "depth", SWAP)
    return update(where, inverses, panels, swap, rhs, parts, other)


def solution(mesh):
    return jax.shard_map(
        per_device,
        mesh=mesh,
        in_specs=(
            P(None, None, ("row", "col"), "depth"),
            P(None, None, "depth", ("row", "col"), None),
            P(),
        ),
        out_specs=P(None, None, ("row", "col"), "depth"),
        check_vma=False,
    )
```

```python
import jax
import jax.numpy as jnp
from jax import lax
from jax.experimental import pallas as pl
from jax.experimental.pallas import tpu as pltpu
from jax.sharding import PartitionSpec as P

BF = jnp.bfloat16
F32 = jnp.float32
SWAP = [(0, 1), (1, 0)]
AXES = ("depth", "row", "col")
SIDE = 4
SHIFTS = (0, 1, 3, 2)
TILES = 4


def place(depth, x, y, z):
    return (depth * 16 + (x % SIDE) * SIDE + y % SIDE) * 8 + z


def plane_groups():
    return [
        [place(d, c // 4, c % 4, z) if d == 0 else place(d, c % 4, c // 4, z) for c in range(16)] for d in range(2) for z in range(8)
    ]


def slow_groups():
    return [
        [place(d, m, o, z) if d == 0 else place(d, o, m, z) for m in range(4)] for d in range(2) for z in range(8) for o in range(4)
    ]


def fast_shift(by):
    return [
        (place(d, x, y, z), place(d, x, y + by, z) if d == 0 else place(d, x + by, y, z))
        for d in range(2)
        for x in range(4)
        for y in range(4)
        for z in range(8)
    ]


def dot(left, right):
    return jnp.dot(left, right, preferred_element_type=F32)


def fill(copies, sems, start=0):
    copies = [pltpu.make_async_copy(source, target, sems.at[start + i]) for i, (source, target) in enumerate(copies)]
    for copy in copies:
        copy.start()
    return copies


def matrix(s, inv_ref, inv):
    return [(inv_ref.at[s, part, :, 256 * k : 256 * k + 256], inv.at[:, 512 * k + 256 * part : 512 * k + 256 * part + 256]) for k in range(2) for part in range(2)]


def half_panel(s, ref, panel):
    return [(ref.at[s, part], panel.at[:, :, 512 * part : 512 * part + 512]) for part in range(2)]


def places(where_ref):
    depth, position = where_ref[0], where_ref[1]
    place_x, place_y = position >> 5, (position >> 3) & 3
    group = jnp.where(depth == 0, place_y, place_x)
    return depth, position, group, place_x + place_y - group


def put(ref, at, back, value):
    rows, columns = value.shape
    for j in range(0, columns, 256):
        real, imag = value[:, j : j + 128], value[:, j + 128 : j + 256]
        ref[at : at + rows, j : j + 128] = real
        ref[at : at + rows, j + 128 : j + 256] = imag
        ref[back : back + rows, j : j + 128] = -imag
        ref[back : back + rows, j + 128 : j + 256] = real


def block(held, s, k):
    return jnp.concatenate(
        [
            jnp.concatenate(
                [ref[m, ((4 * s + zz) * 2 + part) * 32 : ((4 * s + zz) * 2 + part) * 32 + 32, :] for zz in (2 * k, 2 * k + 1) for m in range(4)], axis=0
            )
            for ref in held
            for part in range(2)
        ],
        axis=1,
    )


def solve(inv, work, sol, piece, rows):
    value = dot(inv[:, 0:512], work[0:512])
    low = value[256:] + dot(inv[256:, 512:1024], work[512:1024])
    for at, part in ((0, value[:256]), (256, low)):
        put(sol, at, 512 + at, part.astype(BF))

        @pl.when((rows >> 8) == (at >> 8))
        def _():
            piece[...] = jnp.where((rows & 128) == 0, part[:128], part[128:])


def fill_diag(diag, halves, first):
    for half, shift in zip(halves, SHIFTS):
        at = pl.multiple_of(((first + 4 - shift) & 3) * 128, 128)
        for m in range(4):
            for zz in range(4):
                diag[zz * 128 + m * 32 : zz * 128 + m * 32 + 32, pl.ds(at, 128)] = half[m, zz * 32 : zz * 32 + 32, :]


def load_kernel(where_ref, h0, inv_ref, own_ref, swap_ref, rhs_ref, inv0, inv1, own, swap, state, sol, piece, work, sems):
    depth, position, group, _ = places(where_ref)
    first = fill(matrix(0, inv_ref, inv0) + half_panel(0, own_ref, own.at[0]) + half_panel(0, swap_ref, swap.at[0]), sems)
    rest = [(rhs_ref.at[:, :, :, lanes(group, shift)], state.at[j]) for j, shift in enumerate(SHIFTS)]
    rest = fill(rest + matrix(1, inv_ref, inv1) + half_panel(1, own_ref, own.at[1]) + half_panel(1, swap_ref, swap.at[1]), sems, 8)
    for k in range(2):
        put(work, 512 * k, 512 * k + 256, block([h0], 0, k))
    for copy in first:
        copy.wait()
    solve(inv0, work, sol, piece, (position & 3) * 128)
    for copy in rest:
        copy.wait()
    less(state, state, own.at[0], depth * 3, 0, 3, sol[...], 0)
    less(state, state, swap.at[0], 3 - depth * 3, 0, 3, sol[...], 0)


def lanes(group, shift):
    return pl.ds(pl.multiple_of(((group + 4 - shift) & 3) * 128, 128), 128)


def less(new, old, panel, first, at, count, sol, tile):
    total = dot(panel[at : at + count].reshape(128 * count, 1024), sol)
    cycles = pl.ds(first + at, count)
    for j in range(total.shape[1] // 256):
        for part in range(2):
            place = 256 * j + 128 * part
            new[tile + j, part, cycles] = old[tile + j, part, cycles] - total[:, place : place + 128].reshape(count, 128, 128)


def first_kernel(where_ref, h0, h1, h2, h3, inv0, own, swap, old, known, known_piece, sol, state, left, diag, work, piece):
    depth, position, group, _ = places(where_ref)
    held = (h0, h1, h2, h3)
    for k in range(2):
        put(work, 512 * k, 512 * k + 256, block(held[1:], 0, k))
    fill_diag(diag, [ref.at[:, 512:640] for ref in held], group)
    solve(inv0, work, sol.at[:, 256:], piece, (position & 3) * 128)
    sol[:, :256] = known[...]
    ours = pl.ds(pl.multiple_of(depth * 512, 512), 512)
    for k in range(2):
        left[256 * k : 256 * k + 256] = block(held, 1, k).astype(F32) - dot(diag[256 * k : 256 * k + 256], sol[ours])
    state[0] = old[0]
    less(state, old, own.at[0], depth * 3, 0, 3, sol[:, 256:], 1)
    less(state, old, swap.at[0], 3 - depth * 3, 0, 3, sol[:, 256:], 1)

    @pl.when(position < 4)
    def _():
        for j in range(TILES):
            for part in range(2):
                at = 256 * j + 128 * part
                state[j, part, 0] = known_piece[:, at : at + 128] if j == 0 else piece[:, at - 256 : at - 128]


def second_kernel(where_ref, sol0, state, left, inv, own, swap, half, out_ref, diag, work, sol, piece, new, out_sems):
    depth, position, group, other_group = places(where_ref)
    fill_diag(diag, [half.at[j] for j in range(TILES)], other_group)
    theirs = pl.ds(pl.multiple_of((1 - depth) * 512, 512), 512)
    for k in range(2):
        put(work, 512 * k, 512 * k + 256, (left[256 * k : 256 * k + 256] - dot(diag[256 * k : 256 * k + 256], sol0[theirs])).astype(BF))
    solve(inv, work, sol, piece, (position & 3) * 128)
    stores = []
    for panel, first, at, count in ((own, depth * 3, 0, 3), (swap, 3 - depth * 3, 0, 2), (swap, 3 - depth * 3, 2, 1)):
        less(new, state, panel.at[1], first, at, count, sol[...], 0)
        if at == 0:
            @pl.when((position < 8) & (first == 0))
            def _():
                for j in range(TILES):
                    for part in range(2):
                        place = 256 * j + 128 * part
                        new[j, part, 0] = jnp.where(position < 4, state[j, part, 0], piece[:, place : place + 128])

        cycles = pl.ds(first + at, count)
        stores += fill([(new.at[j, :, cycles], out_ref.at[:, cycles, :, lanes(group, shift)]) for j, shift in enumerate(SHIFTS)], out_sems, len(stores))
    for store in stores:
        store.wait()


def update(where, inverses, own, swap, rhs, held, other):
    smem = pl.BlockSpec(memory_space=pltpu.SMEM)
    hbm = pl.BlockSpec(memory_space=pl.ANY)
    vmem = pl.BlockSpec(memory_space=pltpu.VMEM)

    def call(body, cost, out_shape, scratch, *operands):
        return pl.pallas_call(
            body,
            in_specs=[smem] + [vmem if isinstance(value, list) else hbm for value in operands],
            out_specs=[vmem if isinstance(shape, pl.MemoryRef) else hbm for shape in out_shape],
            out_shape=out_shape,
            scratch_shapes=scratch,
            compiler_params=pltpu.CompilerParams(vmem_limit_bytes=14 * 1024 * 1024),
            cost_estimate=pl.CostEstimate(flops=cost, bytes_accessed=cost // 400, transcendentals=0),
        )(where, *[pltpu.with_memory_space_constraint(value[0], pltpu.VMEM) if isinstance(value, list) else value for value in operands])

    inverses, own, swap, rhs = [pltpu.with_memory_space_constraint(value, pltpu.HBM) for value in (inverses, own, swap, rhs)]
    inverse, half = pltpu.VMEM((512, 1024), BF), pltpu.VMEM((2, 3, 128, 1024), BF)
    state = pltpu.VMEM((TILES, 2, 6, 128, 128), F32)
    inv0, inv1, own, swap, old, known, piece = call(
        load_kernel,
        1_000_000_000,
        [inverse, inverse, half, half, state, pltpu.VMEM((1024, 256), BF), pltpu.VMEM((128, 256), F32)],
        [pltpu.VMEM((1024, 256), BF), pltpu.SemaphoreType.DMA((20,))],
        [held[0]],
        inverses,
        own,
        swap,
        rhs,
    )
    sol, new, left = call(
        first_kernel,
        60_000_000_000,
        [pltpu.VMEM((1024, 1024), BF), state, pltpu.VMEM((512, 1024), F32)],
        [
            pltpu.VMEM((512, 512), BF),
            pltpu.VMEM((1024, 768), BF),
            pltpu.VMEM((128, 768), F32),
        ],
        *[[value] for value in (*held, inv0, own, swap, old, known, piece)],
    )
    (out,) = call(
        second_kernel,
        3_000_000_000,
        [jax.ShapeDtypeStruct(rhs.shape, F32)],
        [
            pltpu.VMEM((512, 512), BF),
            pltpu.VMEM((1024, 1024), BF),
            pltpu.VMEM((1024, 1024), BF),
            pltpu.VMEM((128, 1024), F32),
            state,
            pltpu.SemaphoreType.DMA((16,)),
        ],
        *[[value] for value in (sol, new, left, inv1, own, swap, other)],
    )
    return out


def all_to_all(value, groups):
    return lax.all_to_all(value, AXES, 0, 0, axis_index_groups=groups, tiled=True)


def per_device(rhs, panels, inverses):
    depth = lax.axis_index("depth")
    position = lax.axis_index(("row", "col"))
    where = jnp.stack([depth, position]).astype(jnp.int32)
    swap = lax.ppermute(panels, "depth", SWAP)
    mine = jnp.where(where[0] == 0, lax.optimization_barrier(panels[0, 0, 0]), swap[0, 1, 0])
    rows = rhs[:, 0].astype(BF).reshape(2, 4, 32, 4, 128).transpose(1, 3, 0, 2, 4).reshape(16, 64, 128)
    mine = mine.reshape(4, 32, 4, 128).transpose(0, 2, 1, 3).reshape(16, 32, 128)
    dealt = all_to_all(jnp.concatenate([rows, mine], axis=1), plane_groups())[0]
    line = lax.all_to_all(jnp.broadcast_to(dealt, (8, 96, 128)), "col", 0, 0, tiled=True)
    share = jnp.concatenate([line[:, :64].reshape(512, 128), line[4:, 64:].reshape(128, 128)], axis=0)
    held = all_to_all(jnp.broadcast_to(share, (4, 640, 128)), slow_groups())
    parts = [held] + [lax.ppermute(held, AXES, fast_shift(shift)) for shift in SHIFTS[1:]]
    other = lax.ppermute(jnp.stack([part[:, 512:] for part in parts]), "depth", SWAP)
    return update(where, inverses, panels, swap, rhs, parts, other)


def solution(mesh):
    return jax.shard_map(
        per_device,
        mesh=mesh,
        in_specs=(
            P(None, None, ("row", "col"), "depth"),
            P(None, None, "depth", ("row", "col"), None),
            P(),
        ),
        out_specs=P(None, None, ("row", "col"), "depth"),
        check_vma=False,
    )
```

```python
import jax
import jax.numpy as jnp
from jax import lax
from jax.experimental import pallas as pl
from jax.experimental.pallas import tpu as pltpu
from jax.sharding import PartitionSpec as P

BF = jnp.bfloat16
F32 = jnp.float32
SWAP = [(0, 1), (1, 0)]
AXES = ("depth", "row", "col")
SIDE = 4
SHIFTS = (0, 1, 3, 2)
TILES = 4


def place(depth, x, y, z):
    return (depth * 16 + (x % SIDE) * SIDE + y % SIDE) * 8 + z


def plane_groups():
    return [
        [place(d, c // 4, c % 4, z) if d == 0 else place(d, c % 4, c // 4, z) for c in range(16)] for d in range(2) for z in range(8)
    ]


def slow_groups():
    return [
        [place(d, m, o, z) if d == 0 else place(d, o, m, z) for m in range(4)] for d in range(2) for z in range(8) for o in range(4)
    ]


def fast_shift(by):
    return [
        (place(d, x, y, z), place(d, x, y + by, z) if d == 0 else place(d, x + by, y, z))
        for d in range(2)
        for x in range(4)
        for y in range(4)
        for z in range(8)
    ]


def dot(left, right):
    return jnp.dot(left, right, preferred_element_type=F32)


def fill(copies, sems, start=0):
    copies = [pltpu.make_async_copy(source, target, sems.at[start + i]) for i, (source, target) in enumerate(copies)]
    for copy in copies:
        copy.start()
    return copies


def matrix(s, inv_ref, inv):
    return [(inv_ref.at[s, part, :, 256 * k : 256 * k + 256], inv.at[:, 512 * k + 256 * part : 512 * k + 256 * part + 256]) for k in range(2) for part in range(2)]


def half_panel(s, ref, panel):
    return [(ref.at[s, part], panel.at[:, :, 512 * part : 512 * part + 512]) for part in range(2)]


def places(where_ref):
    depth, position = where_ref[0], where_ref[1]
    place_x, place_y = position >> 5, (position >> 3) & 3
    group = jnp.where(depth == 0, place_y, place_x)
    return depth, position, group, place_x + place_y - group


def put(ref, at, back, value):
    rows, columns = value.shape
    for j in range(0, columns, 256):
        real, imag = value[:, j : j + 128], value[:, j + 128 : j + 256]
        ref[at : at + rows, j : j + 128] = real
        ref[at : at + rows, j + 128 : j + 256] = imag
        ref[back : back + rows, j : j + 128] = -imag
        ref[back : back + rows, j + 128 : j + 256] = real


def block(held, s, k):
    return jnp.concatenate(
        [
            jnp.concatenate(
                [ref[m, ((4 * s + zz) * 2 + part) * 32 : ((4 * s + zz) * 2 + part) * 32 + 32, :] for zz in (2 * k, 2 * k + 1) for m in range(4)], axis=0
            )
            for ref in held
            for part in range(2)
        ],
        axis=1,
    )


def solve(inv, work, sol, piece, rows):
    value = dot(inv[:, 0:512], work[0:512])
    low = value[256:] + dot(inv[256:, 512:1024], work[512:1024])
    for at, part in ((0, value[:256]), (256, low)):
        put(sol, at, 512 + at, part.astype(BF))

        @pl.when((rows >> 8) == (at >> 8))
        def _():
            piece[...] = jnp.where((rows & 128) == 0, part[:128], part[128:])


def fill_diag(diag, halves, first):
    for half, shift in zip(halves, SHIFTS):
        at = pl.multiple_of(((first + 4 - shift) & 3) * 128, 128)
        for m in range(4):
            for zz in range(4):
                diag[zz * 128 + m * 32 : zz * 128 + m * 32 + 32, pl.ds(at, 128)] = half[m, zz * 32 : zz * 32 + 32, :]


def load_kernel(where_ref, h0, inv_ref, own_ref, swap_ref, rhs_ref, inv0, inv1, own, swap, state, sol, piece, work, sems):
    depth, position, group, _ = places(where_ref)
    first = fill(matrix(0, inv_ref, inv0) + half_panel(0, own_ref, own.at[0]) + half_panel(0, swap_ref, swap.at[0]), sems)
    rest = [(rhs_ref.at[:, :, :, lanes(group, shift)], state.at[j]) for j, shift in enumerate(SHIFTS)]
    rest = fill(rest + matrix(1, inv_ref, inv1) + half_panel(1, own_ref, own.at[1]) + half_panel(1, swap_ref, swap.at[1]), sems, 8)
    for k in range(2):
        put(work, 512 * k, 512 * k + 256, block([h0], 0, k))
    for copy in first:
        copy.wait()
    solve(inv0, work, sol, piece, (position & 3) * 128)
    for copy in rest:
        copy.wait()
    less(state, state, own.at[0], depth * 3, 0, 3, sol[...], 0)
    less(state, state, swap.at[0], 3 - depth * 3, 0, 3, sol[...], 0)

    @pl.when(position < 4)
    def _():
        for part in range(2):
            state[0, part, 0] = piece[:, 128 * part : 128 * part + 128]


def lanes(group, shift):
    return pl.ds(pl.multiple_of(((group + 4 - shift) & 3) * 128, 128), 128)


def less(new, old, panel, first, at, count, sol, tile):
    total = dot(panel[at : at + count].reshape(128 * count, 1024), sol)
    cycles = pl.ds(first + at, count)
    for j in range(total.shape[1] // 256):
        for part in range(2):
            place = 256 * j + 128 * part
            new[tile + j, part, cycles] = (old[tile + j] if isinstance(old, list) else old)[tile + j, part, cycles] - total[:, place : place + 128].reshape(count, 128, 128)


def first_kernel(where_ref, h0, h1, h2, h3, inv0, own, swap, old, known, sol, state, left, diag, work, piece):
    depth, position, group, _ = places(where_ref)
    held = (h0, h1, h2, h3)
    for k in range(2):
        put(work, 512 * k, 512 * k + 256, block(held[1:], 0, k))
    fill_diag(diag, [ref.at[:, 512:640] for ref in held], group)
    solve(inv0, work, sol.at[:, 256:], piece, (position & 3) * 128)
    sol[:, :256] = known[...]
    ours = pl.ds(pl.multiple_of(depth * 512, 512), 512)
    for k in range(2):
        left[256 * k : 256 * k + 256] = block(held, 1, k).astype(F32) - dot(diag[256 * k : 256 * k + 256], sol[ours])
    less(state, old, own.at[0], depth * 3, 0, 3, sol[:, 256:], 1)
    less(state, old, swap.at[0], 3 - depth * 3, 0, 3, sol[:, 256:], 1)

    @pl.when(position < 4)
    def _():
        for j in range(1, TILES):
            for part in range(2):
                at = 256 * j + 128 * part
                state[j, part, 0] = piece[:, at - 256 : at - 128]


def second_kernel(where_ref, sol0, old, state, left, inv, own, swap, half, out_ref, diag, work, sol, piece, new, out_sems):
    depth, position, group, other_group = places(where_ref)
    fill_diag(diag, [half.at[j] for j in range(TILES)], other_group)
    theirs = pl.ds(pl.multiple_of((1 - depth) * 512, 512), 512)
    for k in range(2):
        put(work, 512 * k, 512 * k + 256, (left[256 * k : 256 * k + 256] - dot(diag[256 * k : 256 * k + 256], sol0[theirs])).astype(BF))
    solve(inv, work, sol, piece, (position & 3) * 128)
    stores = []
    for panel, first, at, count in ((own, depth * 3, 0, 3), (swap, 3 - depth * 3, 0, 2), (swap, 3 - depth * 3, 2, 1)):
        less(new, [old] + [state] * (TILES - 1), panel.at[1], first, at, count, sol[...], 0)
        if at == 0:
            @pl.when((position < 8) & (first == 0))
            def _():
                for j in range(TILES):
                    for part in range(2):
                        place = 256 * j + 128 * part
                        new[j, part, 0] = jnp.where(position < 4, (state if j else old)[j, part, 0], piece[:, place : place + 128])

        cycles = pl.ds(first + at, count)
        stores += fill([(new.at[j, :, cycles], out_ref.at[:, cycles, :, lanes(group, shift)]) for j, shift in enumerate(SHIFTS)], out_sems, len(stores))
    for store in stores:
        store.wait()


def update(where, inverses, own, swap, rhs, held, other):
    smem = pl.BlockSpec(memory_space=pltpu.SMEM)
    hbm = pl.BlockSpec(memory_space=pl.ANY)
    vmem = pl.BlockSpec(memory_space=pltpu.VMEM)

    def call(body, cost, out_shape, scratch, *operands):
        return pl.pallas_call(
            body,
            in_specs=[smem] + [vmem if isinstance(value, list) else hbm for value in operands],
            out_specs=[vmem if isinstance(shape, pl.MemoryRef) else hbm for shape in out_shape],
            out_shape=out_shape,
            scratch_shapes=scratch,
            compiler_params=pltpu.CompilerParams(vmem_limit_bytes=14 * 1024 * 1024),
            cost_estimate=pl.CostEstimate(flops=cost, bytes_accessed=cost // 400, transcendentals=0),
        )(where, *[pltpu.with_memory_space_constraint(value[0], pltpu.VMEM) if isinstance(value, list) else value for value in operands])

    inverses, own, swap, rhs = [pltpu.with_memory_space_constraint(value, pltpu.HBM) for value in (inverses, own, swap, rhs)]
    inverse, half = pltpu.VMEM((512, 1024), BF), pltpu.VMEM((2, 3, 128, 1024), BF)
    state = pltpu.VMEM((TILES, 2, 6, 128, 128), F32)
    inv0, inv1, own, swap, old, known, _ = call(
        load_kernel,
        1_000_000_000,
        [inverse, inverse, half, half, state, pltpu.VMEM((1024, 256), BF), pltpu.VMEM((128, 256), F32)],
        [pltpu.VMEM((1024, 256), BF), pltpu.SemaphoreType.DMA((20,))],
        [held[0]],
        inverses,
        own,
        swap,
        rhs,
    )
    sol, new, left = call(
        first_kernel,
        60_000_000_000,
        [pltpu.VMEM((1024, 1024), BF), state, pltpu.VMEM((512, 1024), F32)],
        [
            pltpu.VMEM((512, 512), BF),
            pltpu.VMEM((1024, 768), BF),
            pltpu.VMEM((128, 768), F32),
        ],
        *[[value] for value in (*held, inv0, own, swap, old, known)],
    )
    (out,) = call(
        second_kernel,
        3_000_000_000,
        [jax.ShapeDtypeStruct(rhs.shape, F32)],
        [
            pltpu.VMEM((512, 512), BF),
            pltpu.VMEM((1024, 1024), BF),
            pltpu.VMEM((1024, 1024), BF),
            pltpu.VMEM((128, 1024), F32),
            state,
            pltpu.SemaphoreType.DMA((16,)),
        ],
        *[[value] for value in (sol, old, new, left, inv1, own, swap, other)],
    )
    return out


def all_to_all(value, groups):
    return lax.all_to_all(value, AXES, 0, 0, axis_index_groups=groups, tiled=True)


def per_device(rhs, panels, inverses):
    depth = lax.axis_index("depth")
    position = lax.axis_index(("row", "col"))
    where = jnp.stack([depth, position]).astype(jnp.int32)
    swap = lax.ppermute(panels, "depth", SWAP)
    mine = jnp.where(where[0] == 0, lax.optimization_barrier(panels[0, 0, 0]), swap[0, 1, 0])
    rows = rhs[:, 0].astype(BF).reshape(2, 4, 32, 4, 128).transpose(1, 3, 0, 2, 4).reshape(16, 64, 128)
    mine = mine.reshape(4, 32, 4, 128).transpose(0, 2, 1, 3).reshape(16, 32, 128)
    dealt = all_to_all(jnp.concatenate([rows, mine], axis=1), plane_groups())[0]
    line = lax.all_to_all(jnp.broadcast_to(dealt, (8, 96, 128)), "col", 0, 0, tiled=True)
    share = jnp.concatenate([line[:, :64].reshape(512, 128), line[4:, 64:].reshape(128, 128)], axis=0)
    held = all_to_all(jnp.broadcast_to(share, (4, 640, 128)), slow_groups())
    parts = [held] + [lax.ppermute(held, AXES, fast_shift(shift)) for shift in SHIFTS[1:]]
    other = lax.ppermute(jnp.stack([part[:, 512:] for part in parts]), "depth", SWAP)
    return update(where, inverses, panels, swap, rhs, parts, other)


def solution(mesh):
    return jax.shard_map(
        per_device,
        mesh=mesh,
        in_specs=(
            P(None, None, ("row", "col"), "depth"),
            P(None, None, "depth", ("row", "col"), None),
            P(),
        ),
        out_specs=P(None, None, ("row", "col"), "depth"),
        check_vma=False,
    )
```
